32 devices in a mesh: groups: 2 (over y), band: 4 (over z), lon: 2 (over x), mp: 2 (over core).
Axes of the slice: x: 2, y: 2, z: 4, core: 2. Of those that a mesh axis runs over, the one named last changes fastest.
Arguments:
- cycle_field: bfloat16 [128, 83, 3072], P(('groups', 'band'), None, ('lon', 'mp')), parts along dimension 0, may hold values from -6 to 6
- cycle_length: int32 [64], P('band'), may hold values from 768 to 3072, as said below
- metric_weight: float32 [9, 64, 1440], P(None, 'band', ('lon', 'mp')), may hold values from -0.5 to 0.5
- patch_weight: bfloat16 [1328, 1024], P(None, 'mp'), may hold values from -0.15625 to 0.15625
- patch_bias: float32 [1024], P('mp'), may hold values from -4 to 4
- owner: int32 [4, 2, 720, 1], P('band', 'lon'), may hold values from 0 to 3; in each aligned block of 720 rows (0 to 719, 720 to 1439, ..., all dimensions but the last counted through in order) at most 360 rows name the same one
Outputs:
- owned: bfloat16 [8, 2, 4, 360, 1024], P(('groups', 'band'), 'lon', None, None, 'mp'), parts along dimension 0
The draws below stay inside these ranges and needn't reach their ends.
There are 2 independent parts, one for each index of `groups`. The reference program is written for one: setup_inputs(seed, part) draws one part's arguments, and reference() takes and returns one part's arrays. A program takes and returns all parts, laid end to end along the dimension named above; an argument that names none is the same for every part. Nothing has to cross between parts.
Inputs may be any that keep to these rules, and one draw needn't show every extreme that they name: `cycle_length`: the longest cycle has exactly 3072 points in every draw. Within one group of 720 tokens no owner is named more than 360 times.
All inputs are finite; a program needn't handle non-finite values.
Results may differ from the reference program's by a relative error of at most 0.0052.
Values may be sent and summed in bfloat16 or wider, within the bound.
A program may use at most 64 MiB of HBM per device.

```python
import math
import jax
import jax.numpy as jnp
import numpy as np
from jax import lax

CYCLE_DEV = 16
VARS = 83
PTS = 3072
NOUT = 1440
PATCH = 4
WIDTH = 1024
KIN = 1328
CYCLES = 64
TOK_GROUP = 720
CAP = 360
N_BAND = 4
N_LON = 2


def draw_cycle_length(key, part):
    key = jax.random.fold_in(key, 11)
    first, second = jax.random.split(key)
    lengths = jax.random.randint(first, (CYCLES,), PTS // 4, PTS + 1).astype(jnp.int32)
    where = jax.random.randint(second, (), 0, CYCLES)
    return lengths.at[where].set(PTS)


def block_scale(rng, shape, pieces, smallest, largest):
    factor_of, own = 1.0, jax.random.fold_in(rng, 6)
    for dim, parts in pieces:
        draws = jnp.exp(jax.random.uniform(jax.random.fold_in(own, dim), (parts,), jnp.float32, smallest / len(pieces), largest / len(pieces)))
        factor_of = factor_of * jnp.repeat(draws, shape[dim] // parts).reshape([-1 if axis == dim else 1 for axis in range(len(shape))])
    return factor_of


def shared_out(stream_key, own, number, rows, amount, top, reach, slope):
    sequence = jax.random.permutation(stream_key, amount)
    packed, usual = load_shares(amount, rows * top, reach, slope, True), load_shares(amount, rows * top, reach, slope, False)
    places = jnp.arange(amount)

    def named(sizes, offset_by):
        used = int((sizes > 0).sum())
        fixed = max(1, used // 4)
        passed = fixed + (places - fixed + offset_by * (used - fixed)) % max(1, amount - fixed)
        return jnp.zeros((amount,), jnp.int32).at[sequence[jnp.where(places < fixed, places, passed)]].set(jnp.asarray(sizes, jnp.int32))

    sizes = jnp.where(number % 4 == 0, named(packed, number // 4), named(usual, number - number // 4 - 1))
    mixed = jax.random.permutation(jax.random.fold_in(own, 3), amount)
    giver, sink = mixed[0:amount // 2 * 2:2], mixed[1:amount // 2 * 2:2]
    room = jnp.minimum(sizes[giver] - 1, reach - sizes[sink]) // 2
    room = jnp.where((giver == sequence[0]) | (sink == sequence[0]) | (sizes[sink] == 0), 0, jnp.maximum(room, 0))
    passed = jax.random.randint(jax.random.fold_in(own, 4), (amount // 2,), 0, 1 << 20) % (room + 1)
    sizes = sizes.at[giver].add(-passed).at[sink].add(passed)
    members = jnp.searchsorted(jnp.cumsum(sizes), jnp.arange(rows * top), side="right").astype(jnp.int32)
    grid = members.reshape(top, rows).T
    grid = grid[jax.random.permutation(jax.random.fold_in(own, 1), rows)]
    offset_by = jax.random.randint(jax.random.fold_in(own, 2), (rows, 1), 0, top)
    return jnp.take_along_axis(grid, (jnp.arange(top)[None, :] + offset_by) % top, axis=1)


def load_shares(amount, total, bound, slope, full):
    weights = [(1 << 20) // math.isqrt(rank ** slope) + 1 for rank in range(1, amount + 1)]
    largest = bound if full else min(bound, max(-(-total // amount), total * weights[0] // sum(weights)))
    least = 1 if total - largest >= amount - 1 else 0
    counts, surplus = [largest] + [least] * (amount - 1), total - largest - least * (amount - 1)
    while surplus > 0:
        free = [i for i in range(1, amount) if counts[i] < largest] or [i for i in range(1, amount) if counts[i] < bound]
        pool, remaining = sum([weights[i] for i in free]), surplus
        for i in free:
            extra = min(bound - counts[i], max(1, remaining * weights[i] // pool), surplus)
            counts[i] = counts[i] + extra
            surplus = surplus - extra
    return np.array(counts)


def scatter_about(own_key, shape, spread, most, pieces=(), kind=jnp.bfloat16):
    level = block_scale(own_key, shape, pieces, -0.22, 0.18) if pieces else 1.0
    array = jax.random.normal(own_key, shape, jnp.float32) * spread * level
    return jnp.minimum(jnp.maximum(array, -most), most).astype(kind)


def setup_inputs(seed: int = 0, part: int = 0) -> dict:
    key_list = jax.random.split(jax.random.key(seed), 7)
    part_keys = jax.random.split(jax.random.fold_in(key_list[6], part), 7)
    cycle_field = scatter_about(part_keys[0], (CYCLES, VARS, PTS), 1.0, 6.0, ((0, 4), (2, 4)))
    cycle_length = draw_cycle_length(jax.random.fold_in(key_list[6], 71), part)
    metric_weight = jnp.clip(jax.random.uniform(key_list[2], (9, CYCLES, NOUT), jnp.float32, -0.5, 0.5) * block_scale(key_list[2], (9, CYCLES, NOUT), ((1, 4), (2, 4)), -0.4, 0.0), -0.5, 0.5)
    patch_weight = scatter_about(key_list[3], (KIN, WIDTH), KIN ** -0.5, 0.15625, ((1, 2),))
    patch_bias = scatter_about(key_list[4], (WIDTH,), 1.0, 4.0, ((0, 2),), jnp.float32)
    owner_keys = jax.random.split(jax.random.fold_in(key_list[5], 1), N_BAND * N_LON * TOK_GROUP // TOK_GROUP)
    owner_turns = jax.random.permutation(jax.random.fold_in(key_list[5], 3), N_BAND * N_LON * TOK_GROUP // TOK_GROUP)
    owner = jax.vmap(lambda own, number: shared_out(jax.random.fold_in(key_list[5], 2), own, number, TOK_GROUP, N_BAND, 1, CAP, 2))(owner_keys, owner_turns).reshape((N_BAND, N_LON, TOK_GROUP, 1))
    return {"cycle_field": cycle_field, "cycle_length": cycle_length, "metric_weight": metric_weight, "patch_weight": patch_weight, "patch_bias": patch_bias, "owner": owner}


def band_matrix(length, kstart, count, jstart, width):
    kpos = (kstart + jnp.arange(count, dtype=jnp.int32)).astype(jnp.float32)[:, None]
    jpos = (jstart + jnp.arange(width, dtype=jnp.int32)).astype(jnp.float32)[None, :]
    size = length.astype(jnp.float32)
    centre = jpos * size / NOUT
    dist = jnp.abs(kpos - centre)
    dist = jnp.minimum(dist, size - dist)
    weight = jnp.maximum(0.0, 1.0 - dist) * (kpos < size).astype(jnp.float32)
    return weight.astype(jnp.bfloat16)


def reference(cycle_field, cycle_length, metric_weight, patch_weight, patch_bias, owner):
    def one_cycle(item):
        field_row, length = item
        matrix = band_matrix(length, 0, PTS, 0, NOUT)
        return jnp.dot(field_row, matrix, preferred_element_type=jnp.float32).astype(jnp.bfloat16)

    gridded = lax.map(one_cycle, (cycle_field, cycle_length))
    wide = gridded.astype(jnp.float32)
    padded = jnp.pad(wide, ((1, 1), (0, 0), (0, 0)))
    padded = jnp.concatenate([padded[:, :, -1:], padded, padded[:, :, :1]], axis=2)
    total = wide
    for first in range(3):
        for second in range(3):
            shifted = padded[first:first + CYCLES, :, second:second + NOUT]
            total = total + metric_weight[3 * first + second][:, None, :] * shifted
    stenciled = total.astype(jnp.bfloat16)
    prows = CYCLES // PATCH
    pcols = NOUT // PATCH
    patches = stenciled.reshape(prows, PATCH, VARS, pcols, PATCH).transpose(0, 3, 1, 2, 4).reshape(prows * pcols, KIN)
    encoded = (jnp.dot(patches, patch_weight, preferred_element_type=jnp.float32) + patch_bias[None, :]).astype(jnp.bfloat16)
    rows_dev = CYCLE_DEV // PATCH
    cols_lon = NOUT // (PATCH * N_LON)
    encoded = encoded.reshape(N_BAND, rows_dev, N_LON, cols_lon, WIDTH).transpose(0, 2, 1, 3, 4).reshape(N_BAND, N_LON, TOK_GROUP, WIDTH)
    dest = owner[..., 0]
    onehot = (dest[..., None] == jnp.arange(N_BAND, dtype=jnp.int32)).astype(jnp.int32)
    before = jnp.cumsum(onehot, axis=2) - onehot
    slot = jnp.sum(before * onehot, axis=3).astype(jnp.int32)
    src_idx = jnp.broadcast_to(jnp.arange(N_BAND, dtype=jnp.int32)[:, None, None], dest.shape)
    lon_idx = jnp.broadcast_to(jnp.arange(N_LON, dtype=jnp.int32)[None, :, None], dest.shape)
    owned = jnp.zeros((N_BAND, N_LON, N_BAND, CAP, WIDTH), jnp.bfloat16)
    owned = owned.at[dest, lon_idx, src_idx, slot].set(encoded)
    return owned
```

```python
import jax
import jax.numpy as jnp
from jax import lax
from jax.sharding import PartitionSpec as P

NOUT = 1440
PATCH = 4
CHUNKS = 4


def swap(array, axis="mp"):
    return lax.ppermute(array, axis, [(0, 1), (1, 0)])


def column_targets(jstart, stride):
    col = jnp.arange(PATCH * stride, dtype=jnp.int32)
    phase = col // stride
    place = col % stride - (phase == PATCH - 1).astype(jnp.int32)
    return (jstart + PATCH * place + phase + NOUT) % NOUT


def band_matrix(length, kstart, count, jpos):
    kpos = (kstart + jnp.arange(count, dtype=jnp.int32)).astype(jnp.float32)[None, :, None]
    size = length.astype(jnp.float32)[:, None, None]
    centre = jpos.astype(jnp.float32)[None, None, :] * size / NOUT
    dist = jnp.abs(kpos - centre)
    dist = jnp.minimum(dist, size - dist)
    weight = jnp.maximum(0.0, 1.0 - dist) * (kpos < size).astype(jnp.float32)
    return weight.astype(jnp.bfloat16)


def interpolate(field, length, kstart, jpos):
    matrix = band_matrix(length, kstart, field.shape[2], jpos)
    return jnp.einsum("rvk,rkj->rvj", field, matrix, preferred_element_type=jnp.float32).astype(
        jnp.bfloat16
    )


def stencil(padded, weights, stride):
    wide = padded.astype(jnp.float32)
    rows = padded.shape[0] - 2
    phase = jnp.arange(PATCH * stride, dtype=jnp.int32) // stride
    one = jnp.roll(wide, -1, axis=2)
    centre = jnp.where(phase < PATCH - 1, wide, one)
    left = jnp.roll(wide, stride, axis=2)
    right = jnp.where(
        phase < PATCH - 2, jnp.roll(wide, -stride, axis=2), jnp.roll(wide, -stride - 1, axis=2)
    )
    total = centre[1 : rows + 1]
    for first in range(3):
        for second, shifted in enumerate((left, centre, right)):
            total = total + weights[3 * first + second][:, None, :] * shifted[first : first + rows]
    return total.astype(jnp.bfloat16)


def per_device(cycle_field, cycle_length, metric_weight, patch_weight, patch_bias, owner):
    cycle_rows, nvars, pts_local = cycle_field.shape
    cols_local = metric_weight.shape[2]
    cells = cols_local // PATCH
    stride = -(-(cells + 1) * PATCH // 128) * 128 // PATCH
    nlon = lax.axis_size("lon")
    lon, mp = lax.axis_index("lon"), lax.axis_index("mp")
    bands = lax.axis_size("band")
    width = patch_weight.shape[1]
    kstart = (lon * 2 + mp) * pts_local

    kpad = -nvars % 16
    weight4 = patch_weight.reshape(PATCH, nvars, PATCH, width).transpose(0, 2, 1, 3)
    weight4 = jnp.pad(weight4, ((0, 0), (0, 0), (0, kpad), (0, 0)))
    bias = patch_bias[None, :]
    partner_weight = swap(weight4)
    partner_bias = swap(bias)

    metric = metric_weight.reshape(9, cycle_rows, cells, PATCH).transpose(0, 1, 3, 2)
    metric = jnp.pad(metric, ((0, 0), (0, 0), (0, 0), (0, stride - cells)))
    metric = metric.reshape(9, cycle_rows, PATCH * stride)

    def targets(mp_to):
        return jnp.concatenate(
            [
                column_targets(((lon + d) % nlon * 2 + mp_to) * cols_local, stride)
                for d in range(nlon)
            ]
        )

    own_cols, other_cols = targets(mp), targets(1 - mp)
    step = cycle_rows // CHUNKS
    span = PATCH * stride
    gridded = [None] * CHUNKS
    for chunk in [0, CHUNKS - 1] + list(range(1, CHUNKS - 1)):
        field = cycle_field[chunk * step : (chunk + 1) * step]
        length = cycle_length[chunk * step : (chunk + 1) * step]
        sent = swap(interpolate(field, length, kstart, other_cols))
        both = interpolate(field, length, kstart, own_cols) + sent
        total = both[:, :, :span]
        for d in range(1, nlon):
            total = total + lax.ppermute(
                both[:, :, d * span : (d + 1) * span],
                "lon",
                [(i, (i + d) % nlon) for i in range(nlon)],
            )
        gridded[chunk] = total
    up = [(i, i + 1) for i in range(bands - 1)]
    before = lax.ppermute(gridded[-1][-1:], "band", up)
    after = lax.ppermute(gridded[0][:1], "band", [(b, a) for a, b in up])
    padded = jnp.concatenate([before] + gridded + [after], axis=0)
    stenciled = stencil(padded, metric, stride)
    rows_dev = cycle_rows // PATCH
    patches = stenciled.reshape(rows_dev, PATCH, nvars, PATCH, stride)[..., :cells]
    patches = patches.transpose(0, 1, 3, 2, 4)
    patches = jnp.pad(patches, ((0, 0), (0, 0), (0, 0), (0, kpad), (0, 0)))
    patches = patches.reshape(rows_dev, -1, cells)

    def encode(weight, offset):
        out = jnp.einsum(
            "qkc,kw->qcw", patches, weight.reshape(-1, width), preferred_element_type=jnp.float32
        )
        return (out + offset[None]).astype(jnp.bfloat16)

    partner = swap(encode(partner_weight, partner_bias))
    mine = encode(weight4, bias)

    dest = owner.reshape(-1)
    count_tok = dest.shape[0]
    capacity = max(2, 2 * count_tok // bands)
    onehot = (dest[:, None] == jnp.arange(bands, dtype=jnp.int32)[None, :]).astype(jnp.int32)
    earlier = jnp.cumsum(onehot, axis=0) - onehot
    slot = jnp.sum(earlier * onehot, axis=1)
    where = (dest * capacity + slot).reshape(rows_dev, 2, cells)
    lower = mp == 0
    halves = jnp.stack(
        [
            jnp.where(lower, where[:, 0], where[:, 1]),
            jnp.where(lower, where[:, 1], where[:, 0]),
        ]
    ).reshape(-1)
    select = (
        halves[None, :] == jnp.arange(bands * capacity, dtype=jnp.int32)[:, None]
    ).astype(jnp.bfloat16)
    tokens = jnp.concatenate([mine.reshape(-1, width), partner.reshape(-1, width)], axis=0)
    outbox = (
        jnp.dot(select, tokens, preferred_element_type=jnp.float32)
        .astype(jnp.bfloat16)
        .reshape(bands, capacity, width)
    )
    inbox = lax.all_to_all(outbox, "band", split_axis=0, concat_axis=0, tiled=True)
    return inbox.reshape(1, 1, bands, capacity, width)


def solution(mesh):
    return jax.shard_map(
        per_device,
        mesh=mesh,
        in_specs=(
            P(("groups", "band"), None, ("lon", "mp")),
            P("band"),
            P(None, "band", ("lon", "mp")),
            P(None, "mp"),
            P("mp"),
            P("band", "lon", None, None),
        ),
        out_specs=P(("groups", "band"), "lon", None, None, "mp"),
        check_vma=False,
    )
```

```python
import functools

import jax
import jax.numpy as jnp
from jax import lax
from jax.experimental import pallas as pl
from jax.experimental.pallas import tpu as pltpu
from jax.sharding import PartitionSpec as P

NOUT = 1440
PATCH = 4
CHUNKS = 4


def swap(array, axis="mp"):
    return lax.ppermute(array, axis, [(0, 1), (1, 0)])


def interpolate_kernel(nlon, row0, cols, length_ref, place_ref, field_ref, other_ref, own_ref, total):
    nvars, points = field_ref.shape[1:]
    span = own_ref.shape[3]
    stride = span // PATCH
    tile = 256 if points % 256 == 0 else 128
    lon, mp = place_ref[0], place_ref[1]
    kstart = (lon * 2 + mp) * points
    length = length_ref[row0 + pl.program_id(0)]
    size = length.astype(jnp.float32)
    col = lax.broadcasted_iota(jnp.int32, (1, span), 1)
    phase = sum((col >= b * stride).astype(jnp.int32) for b in range(1, PATCH))
    place = col - phase * stride - (phase == PATCH - 1).astype(jnp.int32)
    relative = PATCH * place + phase
    for e in range(2):
        out_ref = other_ref if e else own_ref
        for d in range(nlon):
            target = lax.rem(lon + d, nlon) * 2 + (1 - mp if e else mp)
            jstart = target * cols
            jpos = jstart + relative
            jpos = jnp.where(jpos < 0, jpos + NOUT, jpos)
            jpos = jnp.where(jpos >= NOUT, jpos - NOUT, jpos)
            centre = jpos.astype(jnp.float32) * size / NOUT
            low = (jstart - 1).astype(jnp.float32) * size / NOUT - 2.0
            high = (jstart + cols).astype(jnp.float32) * size / NOUT + 2.0
            total[...] = jnp.zeros_like(total)
            for t in range(points // tile):
                first = kstart + t * tile
                start = first.astype(jnp.float32)
                near = (start <= high) & (start + tile >= low)
                turned = (target == 0) & (start <= size + 2.0) & (start + tile >= size - 6.0)
                closing = (target == 2 * nlon - 1) & (first == 0)

                @pl.when(near | turned | closing)
                def _():
                    kint = first + lax.broadcasted_iota(jnp.int32, (tile, 1), 0)
                    kpos = jnp.where(kint < length, kint.astype(jnp.float32), -1e6)
                    weight = jnp.maximum(1.0 - jnp.abs(kpos - centre), 0.0)
                    total[...] += jnp.dot(
                        field_ref[0, :, t * tile : (t + 1) * tile],
                        weight.astype(jnp.bfloat16),
                        preferred_element_type=jnp.float32,
                    )

            @pl.when(kstart == 0)
            def _():
                wrap = jnp.maximum(1.0 - (size - centre), 0.0)
                wrap = wrap.astype(jnp.bfloat16).astype(jnp.float32)
                total[...] += field_ref[0, :, 0:128].astype(jnp.float32)[:, 0:1] * wrap

            out_ref[d, 0] = total[...].astype(jnp.bfloat16)


def interpolate(field, length, place, chunk, rows, nlon, cols, span):
    nvars, points = field.shape[1:]
    out = jax.ShapeDtypeStruct((nlon, rows, nvars, span), jnp.bfloat16)
    out_spec = pl.BlockSpec((nlon, 1, nvars, span), lambda r, *_: (0, r, 0, 0))
    return pl.pallas_call(
        functools.partial(interpolate_kernel, nlon, chunk * rows, cols),
        out_shape=(out, out),
        grid_spec=pltpu.PrefetchScalarGridSpec(
            num_scalar_prefetch=2,
            grid=(rows,),
            in_specs=[pl.BlockSpec((1, nvars, points), lambda r, *_: (chunk * rows + r, 0, 0))],
            out_specs=(out_spec, out_spec),
            scratch_shapes=[pltpu.VMEM((nvars, span), jnp.float32)],
        ),
        cost_estimate=pl.CostEstimate(
            flops=4 * nlon * rows * nvars * points * span,
            bytes_accessed=rows * nvars * (2 * points + 8 * nlon * span),
            transcendentals=0,
        ),
        name="interpolate",
    )(length, place, field)


def encode_kernel(nchunks, cells, *refs):
    chunk_refs, (before_ref, after_ref) = refs[:nchunks], refs[nchunks : nchunks + 2]
    metric_ref, weight_a, weight_b, bias_a, bias_b, out_a, out_b, patches = refs[nchunks + 2 :]
    step, nvars, span = chunk_refs[0].shape
    stride = span // PATCH
    rows = nchunks * step
    lanes = patches.shape[1]
    vpad = patches.shape[0] // (PATCH * PATCH)
    phase_at = lax.broadcasted_iota(jnp.int32, (1, span), 1)

    def views(row):
        if row < 0:
            block = before_ref[0]
        elif row >= rows:
            block = after_ref[0]
        else:
            block = chunk_refs[row // step][row % step]
        wide = block.astype(jnp.float32)
        centre = jnp.where(
            phase_at < (PATCH - 1) * stride, wide, pltpu.roll(wide, span - 1, 1)
        )
        left = pltpu.roll(wide, stride, 1)
        right = jnp.where(
            phase_at < (PATCH - 2) * stride,
            pltpu.roll(wide, span - stride, 1),
            pltpu.roll(wide, span - stride - 1, 1),
        )
        return left, centre, right

    patches[...] = jnp.zeros_like(patches)
    window = [views(-1), views(0), None]
    for q in range(rows // PATCH):
        for a in range(PATCH):
            row = q * PATCH + a
            window[2] = views(row + 1)
            result = window[1][1]
            for first in range(3):
                for second in range(3):
                    coeff = metric_ref[3 * first + second, row : row + 1, :]
                    result = result + coeff * window[first][second]
            window = [window[1], window[2], None]
            for b in range(PATCH):
                moved = pltpu.roll(result, (span - b * stride) % span, 1) if b else result
                base = (a * PATCH + b) * vpad
                patches[base : base + nvars, :] = moved[:, :lanes].astype(jnp.bfloat16)
        tokens = patches[...].T
        for weight, bias, out in ((weight_b, bias_b, out_b), (weight_a, bias_a, out_a)):
            value = jnp.dot(tokens, weight[...], preferred_element_type=jnp.float32) + bias[...]
            out[q] = value[:cells].astype(jnp.bfloat16)


def encode(chunks, before, after, metric, weights, biases, cells):
    step, nvars, span = chunks[0].shape
    rows_dev = len(chunks) * step // PATCH
    depth, width = weights[0].shape
    out = jax.ShapeDtypeStruct((rows_dev, cells, width), jnp.bfloat16)
    vmem = pl.BlockSpec(memory_space=pltpu.VMEM)
    return pl.pallas_call(
        functools.partial(encode_kernel, len(chunks), cells),
        out_shape=(out, out),
        in_specs=[vmem] * (len(chunks) + 7),
        out_specs=(vmem, vmem),
        scratch_shapes=[pltpu.VMEM((depth, -(-cells // 128) * 128), jnp.bfloat16)],
        compiler_params=pltpu.CompilerParams(vmem_limit_bytes=40 * 1024 * 1024),
        name="encode",
    )(*chunks, before, after, metric, *weights, *biases)


def per_device(cycle_field, cycle_length, metric_weight, patch_weight, patch_bias, owner):
    cycle_rows, nvars, pts_local = cycle_field.shape
    cols_local = metric_weight.shape[2]
    cells = cols_local // PATCH
    stride = -(-(cells + 1) * PATCH // 128) * 128 // PATCH
    nlon = lax.axis_size("lon")
    lon, mp = lax.axis_index("lon"), lax.axis_index("mp")
    bands = lax.axis_size("band")
    width = patch_weight.shape[1]

    kpad = -nvars % 16
    weight4 = patch_weight.reshape(PATCH, nvars, PATCH, width).transpose(0, 2, 1, 3)
    weight4 = jnp.pad(weight4, ((0, 0), (0, 0), (0, kpad), (0, 0)))
    bias = patch_bias[None, :]
    partner_weight = swap(weight4)
    partner_bias = swap(bias)

    metric = metric_weight.reshape(9, cycle_rows, cells, PATCH).transpose(0, 1, 3, 2)
    metric = jnp.pad(metric, ((0, 0), (0, 0), (0, 0), (0, stride - cells)))
    metric = metric.reshape(9, cycle_rows, PATCH * stride)

    step = cycle_rows // CHUNKS
    span = PATCH * stride
    place = jnp.stack([lon, mp]).astype(jnp.int32)
    gridded = [None] * CHUNKS
    for chunk in [0, CHUNKS - 1] + list(range(1, CHUNKS - 1)):
        other, own = interpolate(
            cycle_field, cycle_length, place, chunk, step, nlon, cols_local, span
        )
        sent = swap(other)
        total = own[0] + sent[0]
        for d in range(1, nlon):
            total = total + lax.ppermute(
                own[d] + sent[d], "lon", [(i, (i + d) % nlon) for i in range(nlon)]
            )
        gridded[chunk] = total
    up = [(i, i + 1) for i in range(bands - 1)]
    before = lax.ppermute(gridded[-1][-1:], "band", up)
    after = lax.ppermute(gridded[0][:1], "band", [(b, a) for a, b in up])
    rows_dev = cycle_rows // PATCH
    mine, others = encode(
        gridded,
        before,
        after,
        metric,
        (weight4.reshape(-1, width), partner_weight.reshape(-1, width)),
        (bias, partner_bias),
        cells,
    )
    partner = swap(others)

    dest = owner.reshape(-1)
    count_tok = dest.shape[0]
    capacity = max(2, 2 * count_tok // bands)
    onehot = (dest[:, None] == jnp.arange(bands, dtype=jnp.int32)[None, :]).astype(jnp.int32)
    earlier = jnp.cumsum(onehot, axis=0) - onehot
    slot = jnp.sum(earlier * onehot, axis=1)
    where = (dest * capacity + slot).reshape(rows_dev, 2, cells)
    lower = mp == 0
    halves = jnp.stack(
        [
            jnp.where(lower, where[:, 0], where[:, 1]),
            jnp.where(lower, where[:, 1], where[:, 0]),
        ]
    ).reshape(-1)
    select = (
        halves[None, :] == jnp.arange(bands * capacity, dtype=jnp.int32)[:, None]
    ).astype(jnp.bfloat16)
    tokens = jnp.concatenate([mine.reshape(-1, width), partner.reshape(-1, width)], axis=0)
    outbox = (
        jnp.dot(select, tokens, preferred_element_type=jnp.float32)
        .astype(jnp.bfloat16)
        .reshape(bands, capacity, width)
    )
    inbox = lax.all_to_all(outbox, "band", split_axis=0, concat_axis=0, tiled=True)
    return inbox.reshape(1, 1, bands, capacity, width)


def solution(mesh):
    return jax.shard_map(
        per_device,
        mesh=mesh,
        in_specs=(
            P(("groups", "band"), None, ("lon", "mp")),
            P("band"),
            P(None, "band", ("lon", "mp")),
            P(None, "mp"),
            P("mp"),
            P("band", "lon", None, None),
        ),
        out_specs=P(("groups", "band"), "lon", None, None, "mp"),
        check_vma=False,
    )
```

```python
import functools

import jax
import jax.numpy as jnp
from jax import lax
from jax.experimental import pallas as pl
from jax.experimental.pallas import tpu as pltpu
from jax.sharding import PartitionSpec as P

NOUT = 1440
PATCH = 4
CHUNKS = 4


def swap(array, axis="mp"):
    return lax.ppermute(array, axis, [(0, 1), (1, 0)])


def interpolate_kernel(nlon, row0, cols, length_ref, place_ref, field_ref, *refs):
    nvars, points = field_ref.shape[1:]
    out_refs, total = refs[:-1], refs[-1]
    span = total.shape[1]
    stride = span // PATCH
    tile = 256 if points % 256 == 0 else 128
    lon, mp = place_ref[0], place_ref[1]
    kstart = (lon * 2 + mp) * points
    length = length_ref[row0 + pl.program_id(0)]
    size = length.astype(jnp.float32)
    col = lax.broadcasted_iota(jnp.int32, (1, span), 1)
    phase = sum((col >= b * stride).astype(jnp.int32) for b in range(1, PATCH))
    place = col - phase * stride - (phase == PATCH - 1).astype(jnp.int32)
    relative = PATCH * place + phase
    for e in range(2):
        for d in range(nlon):
            target = lax.rem(lon + d, nlon) * 2 + (1 - mp if e else mp)
            jstart = target * cols
            jpos = jstart + relative
            jpos = jnp.where(jpos < 0, jpos + NOUT, jpos)
            jpos = jnp.where(jpos >= NOUT, jpos - NOUT, jpos)
            centre = jpos.astype(jnp.float32) * size / NOUT
            low = (jstart - 1).astype(jnp.float32) * size / NOUT - 2.0
            high = (jstart + cols).astype(jnp.float32) * size / NOUT + 2.0
            total[...] = jnp.zeros_like(total)
            for t in range(points // tile):
                first = kstart + t * tile
                start = first.astype(jnp.float32)
                near = (start <= high) & (start + tile >= low)
                turned = (target == 0) & (start <= size + 2.0) & (start + tile >= size - 6.0)
                closing = (target == 2 * nlon - 1) & (first == 0)

                @pl.when(near | turned | closing)
                def _():
                    kint = first + lax.broadcasted_iota(jnp.int32, (tile, 1), 0)
                    kpos = jnp.where(kint < length, kint.astype(jnp.float32), -1e6)
                    weight = jnp.maximum(1.0 - jnp.abs(kpos - centre), 0.0)
                    total[...] += jnp.dot(
                        field_ref[0, :, t * tile : (t + 1) * tile],
                        weight.astype(jnp.bfloat16),
                        preferred_element_type=jnp.float32,
                    )

            edge = (target == 0) | (target == 2 * nlon - 1)

            @pl.when((kstart == 0) & (length < NOUT) & edge)
            def _():
                wrap = jnp.maximum(1.0 - (size - centre), 0.0)
                wrap = wrap.astype(jnp.bfloat16).astype(jnp.float32)
                total[...] += field_ref[0, :, 0:128].astype(jnp.float32)[:, 0:1] * wrap

            out_refs[e * nlon + d][0] = total[...].astype(jnp.bfloat16)


def interpolate(field, length, place, chunk, rows, nlon, cols, span):
    nvars, points = field.shape[1:]
    out = jax.ShapeDtypeStruct((rows, nvars, span), jnp.bfloat16)
    out_spec = pl.BlockSpec((1, nvars, span), lambda r, *_: (r, 0, 0))
    return pl.pallas_call(
        functools.partial(interpolate_kernel, nlon, chunk * rows, cols),
        out_shape=(out,) * (2 * nlon),
        grid_spec=pltpu.PrefetchScalarGridSpec(
            num_scalar_prefetch=2,
            grid=(rows,),
            in_specs=[pl.BlockSpec((1, nvars, points), lambda r, *_: (chunk * rows + r, 0, 0))],
            out_specs=(out_spec,) * (2 * nlon),
            scratch_shapes=[pltpu.VMEM((nvars, span), jnp.float32)],
        ),
        cost_estimate=pl.CostEstimate(
            flops=32 * nlon * rows * nvars * points * span,
            bytes_accessed=rows * nvars * (2 * points + 8 * nlon * span),
            transcendentals=0,
        ),
        name="interpolate",
    )(length, place, field)


def encode_kernel(nchunks, cells, *refs):
    chunk_refs, (before_ref, after_ref) = refs[:nchunks], refs[nchunks : nchunks + 2]
    metric_ref, weight_a, weight_b, bias_a, bias_b, out_a, out_b, patches = refs[nchunks + 2 :]
    step, nvars, span = chunk_refs[0].shape
    stride = span // PATCH
    rows = nchunks * step
    lanes = patches.shape[1]
    vpad = patches.shape[0] // (PATCH * PATCH)
    phase_at = lax.broadcasted_iota(jnp.int32, (1, span), 1)

    def views(row):
        if row < 0:
            block = before_ref[0]
        elif row >= rows:
            block = after_ref[0]
        else:
            block = chunk_refs[row // step][row % step]
        wide = block.astype(jnp.float32)
        centre = jnp.where(
            phase_at < (PATCH - 1) * stride, wide, pltpu.roll(wide, span - 1, 1)
        )
        left = pltpu.roll(wide, stride, 1)
        right = jnp.where(
            phase_at < (PATCH - 2) * stride,
            pltpu.roll(wide, span - stride, 1),
            pltpu.roll(wide, span - stride - 1, 1),
        )
        return left, centre, right

    patches[...] = jnp.zeros_like(patches)
    window = [views(-1), views(0), None]
    for q in range(rows // PATCH):
        for a in range(PATCH):
            row = q * PATCH + a
            window[2] = views(row + 1)
            result = window[1][1]
            for first in range(3):
                for second in range(3):
                    coeff = metric_ref[3 * first + second, row : row + 1, :]
                    result = result + coeff * window[first][second]
            window = [window[1], window[2], None]
            for b in range(PATCH):
                moved = pltpu.roll(result, (span - b * stride) % span, 1) if b else result
                base = (a * PATCH + b) * vpad
                patches[base : base + nvars, :] = moved[:, :lanes].astype(jnp.bfloat16)
        tokens = patches[...].T
        for weight, bias, out in ((weight_b, bias_b, out_b), (weight_a, bias_a, out_a)):
            value = jnp.dot(tokens, weight[...], preferred_element_type=jnp.float32) + bias[...]
            out[q] = value[:cells].astype(jnp.bfloat16)


def encode(chunks, before, after, metric, weights, biases, cells):
    step, nvars, span = chunks[0].shape
    rows_dev = len(chunks) * step // PATCH
    depth, width = weights[0].shape
    out = jax.ShapeDtypeStruct((rows_dev, cells, width), jnp.bfloat16)
    vmem = pl.BlockSpec(memory_space=pltpu.VMEM)
    return pl.pallas_call(
        functools.partial(encode_kernel, len(chunks), cells),
        out_shape=(out, out),
        in_specs=[vmem] * (len(chunks) + 7),
        out_specs=(vmem, vmem),
        scratch_shapes=[pltpu.VMEM((depth, -(-cells // 128) * 128), jnp.bfloat16)],
        compiler_params=pltpu.CompilerParams(vmem_limit_bytes=40 * 1024 * 1024),
        name="encode",
    )(*chunks, before, after, metric, *weights, *biases)


def per_device(cycle_field, cycle_length, metric_weight, patch_weight, patch_bias, owner):
    cycle_rows, nvars, pts_local = cycle_field.shape
    cols_local = metric_weight.shape[2]
    cells = cols_local // PATCH
    stride = -(-(cells + 1) * PATCH // 128) * 128 // PATCH
    nlon = lax.axis_size("lon")
    lon, mp = lax.axis_index("lon"), lax.axis_index("mp")
    bands = lax.axis_size("band")
    width = patch_weight.shape[1]

    kpad = -nvars % 16
    weight4 = patch_weight.reshape(PATCH, nvars, PATCH, width).transpose(0, 2, 1, 3)
    weight4 = jnp.pad(weight4, ((0, 0), (0, 0), (0, kpad), (0, 0)))
    bias = patch_bias[None, :]
    partner_weight = swap(weight4)
    partner_bias = swap(bias)

    metric = metric_weight.reshape(9, cycle_rows, cells, PATCH).transpose(0, 1, 3, 2)
    metric = jnp.pad(metric, ((0, 0), (0, 0), (0, 0), (0, stride - cells)))
    metric = metric.reshape(9, cycle_rows, PATCH * stride)

    step = cycle_rows // CHUNKS
    span = PATCH * stride
    place = jnp.stack([lon, mp]).astype(jnp.int32)
    order = [0, CHUNKS - 1] + list(range(1, CHUNKS - 1))
    messages = [None] * CHUNKS
    for index, chunk in enumerate(order):
        if index >= 2:
            place, messages[order[index - 2]] = lax.optimization_barrier(
                (place, messages[order[index - 2]])
            )
        blocks = interpolate(
            cycle_field, cycle_length, place, chunk, step, nlon, cols_local, span
        )
        sent = [swap(block) for block in blocks[nlon:]]
        messages[chunk] = [own + got for own, got in zip(blocks[:nlon], sent)]
    gridded = [None] * CHUNKS
    for chunk in order:
        total = messages[chunk][0]
        for d in range(1, nlon):
            total = total + lax.ppermute(
                messages[chunk][d], "lon", [(i, (i + d) % nlon) for i in range(nlon)]
            )
        gridded[chunk] = total
    up = [(i, i + 1) for i in range(bands - 1)]
    before = lax.ppermute(gridded[-1][-1:], "band", up)
    after = lax.ppermute(gridded[0][:1], "band", [(b, a) for a, b in up])
    rows_dev = cycle_rows // PATCH
    mine, others = encode(
        gridded,
        before,
        after,
        metric,
        (weight4.reshape(-1, width), partner_weight.reshape(-1, width)),
        (bias, partner_bias),
        cells,
    )
    partner = swap(others)

    dest = owner.reshape(-1)
    count_tok = dest.shape[0]
    capacity = max(2, 2 * count_tok // bands)
    onehot = (dest[:, None] == jnp.arange(bands, dtype=jnp.int32)[None, :]).astype(jnp.int32)
    earlier = jnp.cumsum(onehot, axis=0) - onehot
    slot = jnp.sum(earlier * onehot, axis=1)
    where = (dest * capacity + slot).reshape(rows_dev, 2, cells)
    lower = mp == 0
    halves = jnp.stack(
        [
            jnp.where(lower, where[:, 0], where[:, 1]),
            jnp.where(lower, where[:, 1], where[:, 0]),
        ]
    ).reshape(-1)
    select = (
        halves[None, :] == jnp.arange(bands * capacity, dtype=jnp.int32)[:, None]
    ).astype(jnp.bfloat16)
    tokens = jnp.concatenate([mine.reshape(-1, width), partner.reshape(-1, width)], axis=0)
    outbox = (
        jnp.dot(select, tokens, preferred_element_type=jnp.float32)
        .astype(jnp.bfloat16)
        .reshape(bands, capacity, width)
    )
    inbox = lax.all_to_all(outbox, "band", split_axis=0, concat_axis=0, tiled=True)
    return inbox.reshape(1, 1, bands, capacity, width)


def solution(mesh):
    return jax.shard_map(
        per_device,
        mesh=mesh,
        in_specs=(
            P(("groups", "band"), None, ("lon", "mp")),
            P("band"),
            P(None, "band", ("lon", "mp")),
            P(None, "mp"),
            P("mp"),
            P("band", "lon", None, None),
        ),
        out_specs=P(("groups", "band"), "lon", None, None, "mp"),
        check_vma=False,
    )
```

```python
import functools

import jax
import jax.numpy as jnp
from jax import lax
from jax.experimental import pallas as pl
from jax.experimental.pallas import tpu as pltpu
from jax.sharding import PartitionSpec as P

NOUT = 1440
PATCH = 4
CHUNKS = 4


def swap(array, axis="mp"):
    return lax.ppermute(array, axis, [(0, 1), (1, 0)])


def column_targets(jstart, stride):
    col = jnp.arange(PATCH * stride, dtype=jnp.int32)
    phase = col // stride
    place = col % stride - (phase == PATCH - 1).astype(jnp.int32)
    return (jstart + PATCH * place + phase + NOUT) % NOUT


def band_matrix(length, kstart, count, jpos):
    kpos = (kstart + jnp.arange(count, dtype=jnp.int32)).astype(jnp.float32)[None, :, None]
    size = length.astype(jnp.float32)[:, None, None]
    centre = jpos.astype(jnp.float32)[None, None, :] * size / NOUT
    dist = jnp.abs(kpos - centre)
    dist = jnp.minimum(dist, size - dist)
    weight = jnp.maximum(0.0, 1.0 - dist) * (kpos < size).astype(jnp.float32)
    return weight.astype(jnp.bfloat16)


def interpolate(field, length, kstart, jpos):
    matrix = band_matrix(length, kstart, field.shape[2], jpos)
    return jnp.einsum("rvk,rkj->rvj", field, matrix, preferred_element_type=jnp.float32).astype(
        jnp.bfloat16
    )


def encode_kernel(nchunks, cells, *refs):
    chunk_refs, (before_ref, after_ref) = refs[:nchunks], refs[nchunks : nchunks + 2]
    metric_ref, weight_a, weight_b, bias_a, bias_b, out_a, out_b, patches = refs[nchunks + 2 :]
    step, nvars, span = chunk_refs[0].shape
    stride = span // PATCH
    rows = nchunks * step
    lanes = patches.shape[1]
    vpad = patches.shape[0] // (PATCH * PATCH)
    phase_at = lax.broadcasted_iota(jnp.int32, (1, span), 1)

    def views(row):
        if row < 0:
            block = before_ref[0]
        elif row >= rows:
            block = after_ref[0]
        else:
            block = chunk_refs[row // step][row % step]
        wide = block.astype(jnp.float32)
        centre = jnp.where(
            phase_at < (PATCH - 1) * stride, wide, pltpu.roll(wide, span - 1, 1)
        )
        left = pltpu.roll(wide, stride, 1)
        right = jnp.where(
            phase_at < (PATCH - 2) * stride,
            pltpu.roll(wide, span - stride, 1),
            pltpu.roll(wide, span - stride - 1, 1),
        )
        return left, centre, right

    patches[...] = jnp.zeros_like(patches)
    window = [views(-1), views(0), None]
    for q in range(rows // PATCH):
        for a in range(PATCH):
            row = q * PATCH + a
            window[2] = views(row + 1)
            result = window[1][1]
            for first in range(3):
                for second in range(3):
                    coeff = metric_ref[3 * first + second, row : row + 1, :]
                    result = result + coeff * window[first][second]
            window = [window[1], window[2], None]
            for b in range(PATCH):
                moved = pltpu.roll(result, (span - b * stride) % span, 1) if b else result
                base = (a * PATCH + b) * vpad
                patches[base : base + nvars, :] = moved[:, :lanes].astype(jnp.bfloat16)
        tokens = patches[...].T
        for weight, bias, out in ((weight_b, bias_b, out_b), (weight_a, bias_a, out_a)):
            value = jnp.dot(tokens, weight[...], preferred_element_type=jnp.float32) + bias[...]
            out[q] = value[:cells].astype(jnp.bfloat16)


def encode(chunks, before, after, metric, weights, biases, cells):
    step, nvars, span = chunks[0].shape
    rows_dev = len(chunks) * step // PATCH
    depth, width = weights[0].shape
    out = jax.ShapeDtypeStruct((rows_dev, cells, width), jnp.bfloat16)
    vmem = pl.BlockSpec(memory_space=pltpu.VMEM)
    return pl.pallas_call(
        functools.partial(encode_kernel, len(chunks), cells),
        out_shape=(out, out),
        in_specs=[vmem] * (len(chunks) + 7),
        out_specs=(vmem, vmem),
        scratch_shapes=[pltpu.VMEM((depth, -(-cells // 128) * 128), jnp.bfloat16)],
        compiler_params=pltpu.CompilerParams(vmem_limit_bytes=40 * 1024 * 1024),
        name="encode",
    )(*chunks, before, after, metric, *weights, *biases)


def per_device(cycle_field, cycle_length, metric_weight, patch_weight, patch_bias, owner):
    cycle_rows, nvars, pts_local = cycle_field.shape
    cols_local = metric_weight.shape[2]
    cells = cols_local // PATCH
    stride = -(-(cells + 1) * PATCH // 128) * 128 // PATCH
    nlon = lax.axis_size("lon")
    lon, mp = lax.axis_index("lon"), lax.axis_index("mp")
    bands = lax.axis_size("band")
    kstart = (lon * 2 + mp) * pts_local
    width = patch_weight.shape[1]

    kpad = -nvars % 16
    weight4 = patch_weight.reshape(PATCH, nvars, PATCH, width).transpose(0, 2, 1, 3)
    weight4 = jnp.pad(weight4, ((0, 0), (0, 0), (0, kpad), (0, 0)))
    bias = patch_bias[None, :]
    partner_weight = swap(weight4)
    partner_bias = swap(bias)

    metric = metric_weight.reshape(9, cycle_rows, cells, PATCH).transpose(0, 1, 3, 2)
    metric = jnp.pad(metric, ((0, 0), (0, 0), (0, 0), (0, stride - cells)))
    metric = metric.reshape(9, cycle_rows, PATCH * stride)

    def targets(mp_to):
        return jnp.concatenate(
            [
                column_targets(((lon + d) % nlon * 2 + mp_to) * cols_local, stride)
                for d in range(nlon)
            ]
        )

    own_cols, other_cols = targets(mp), targets(1 - mp)
    step = cycle_rows // CHUNKS
    span = PATCH * stride
    gridded = [None] * CHUNKS
    for chunk in [0, CHUNKS - 1] + list(range(1, CHUNKS - 1)):
        field = cycle_field[chunk * step : (chunk + 1) * step]
        length = cycle_length[chunk * step : (chunk + 1) * step]
        sent = swap(interpolate(field, length, kstart, other_cols))
        both = interpolate(field, length, kstart, own_cols) + sent
        total = both[:, :, :span]
        for d in range(1, nlon):
            total = total + lax.ppermute(
                both[:, :, d * span : (d + 1) * span],
                "lon",
                [(i, (i + d) % nlon) for i in range(nlon)],
            )
        gridded[chunk] = total
    up = [(i, i + 1) for i in range(bands - 1)]
    before = lax.ppermute(gridded[-1][-1:], "band", up)
    after = lax.ppermute(gridded[0][:1], "band", [(b, a) for a, b in up])
    rows_dev = cycle_rows // PATCH
    mine, others = encode(
        gridded,
        before,
        after,
        metric,
        (weight4.reshape(-1, width), partner_weight.reshape(-1, width)),
        (bias, partner_bias),
        cells,
    )
    partner = swap(others)

    dest = owner.reshape(-1)
    count_tok = dest.shape[0]
    capacity = max(2, 2 * count_tok // bands)
    onehot = (dest[:, None] == jnp.arange(bands, dtype=jnp.int32)[None, :]).astype(jnp.int32)
    earlier = jnp.cumsum(onehot, axis=0) - onehot
    slot = jnp.sum(earlier * onehot, axis=1)
    where = (dest * capacity + slot).reshape(rows_dev, 2, cells)
    lower = mp == 0
    halves = jnp.stack(
        [
            jnp.where(lower, where[:, 0], where[:, 1]),
            jnp.where(lower, where[:, 1], where[:, 0]),
        ]
    ).reshape(-1)
    select = (
        halves[None, :] == jnp.arange(bands * capacity, dtype=jnp.int32)[:, None]
    ).astype(jnp.bfloat16)
    tokens = jnp.concatenate([mine.reshape(-1, width), partner.reshape(-1, width)], axis=0)
    outbox = (
        jnp.dot(select, tokens, preferred_element_type=jnp.float32)
        .astype(jnp.bfloat16)
        .reshape(bands, capacity, width)
    )
    inbox = lax.all_to_all(outbox, "band", split_axis=0, concat_axis=0, tiled=True)
    return inbox.reshape(1, 1, bands, capacity, width)


def solution(mesh):
    return jax.shard_map(
        per_device,
        mesh=mesh,
        in_specs=(
            P(("groups", "band"), None, ("lon", "mp")),
            P("band"),
            P(None, "band", ("lon", "mp")),
            P(None, "mp"),
            P("mp"),
            P("band", "lon", None, None),
        ),
        out_specs=P(("groups", "band"), "lon", None, None, "mp"),
        check_vma=False,
    )
```

```python
import functools

import jax
import jax.numpy as jnp
from jax import lax
from jax.experimental import pallas as pl
from jax.experimental.pallas import tpu as pltpu
from jax.sharding import PartitionSpec as P

NOUT = 1440
PATCH = 4
CHUNKS = 4


def swap(array, axis="mp"):
    return lax.ppermute(array, axis, [(0, 1), (1, 0)])


def column_targets(jstart, stride):
    col = jnp.arange(PATCH * stride, dtype=jnp.int32)
    phase = col // stride
    place = col % stride - (phase == PATCH - 1).astype(jnp.int32)
    return (jstart + PATCH * place + phase + NOUT) % NOUT


def band_matrix(length, kstart, count, jpos):
    kpos = (kstart + jnp.arange(count, dtype=jnp.int32)).astype(jnp.float32)[None, :, None]
    size = length.astype(jnp.float32)[:, None, None]
    centre = jpos.astype(jnp.float32)[None, None, :] * size / NOUT
    dist = jnp.abs(kpos - centre)
    dist = jnp.minimum(dist, size - dist)
    weight = jnp.maximum(0.0, 1.0 - dist) * (kpos < size).astype(jnp.float32)
    return weight.astype(jnp.bfloat16)


def interpolate(field, length, kstart, jpos):
    matrix = band_matrix(length, kstart, field.shape[2], jpos)
    return jnp.einsum("rvk,rkj->rvj", field, matrix, preferred_element_type=jnp.float32).astype(
        jnp.bfloat16
    )


def encode_kernel(nchunks, cells, *refs):
    chunk_refs, (before_ref, after_ref) = refs[:nchunks], refs[nchunks : nchunks + 2]
    metric_ref, weight_a, weight_b, bias_a, bias_b, out_a, out_b, patches = refs[nchunks + 2 :]
    step, nvars, span = chunk_refs[0].shape
    stride = span // PATCH
    rows = nchunks * step
    lanes = patches.shape[1]
    vpad = patches.shape[0] // (PATCH * PATCH)
    phase_at = lax.broadcasted_iota(jnp.int32, (1, span), 1)

    def views(row):
        if row < 0:
            block = before_ref[0]
        elif row >= rows:
            block = after_ref[0]
        else:
            block = chunk_refs[row // step][row % step]
        wide = block.astype(jnp.float32)
        centre = jnp.where(
            phase_at < (PATCH - 1) * stride, wide, pltpu.roll(wide, span - 1, 1)
        )
        left = pltpu.roll(wide, stride, 1)
        right = jnp.where(
            phase_at < (PATCH - 2) * stride,
            pltpu.roll(wide, span - stride, 1),
            pltpu.roll(wide, span - stride - 1, 1),
        )
        return left, centre, right

    patches[...] = jnp.zeros_like(patches)
    window = [views(-1), views(0), None]
    for q in range(rows // PATCH):
        for a in range(PATCH):
            row = q * PATCH + a
            window[2] = views(row + 1)
            result = window[1][1]
            for first in range(3):
                for second in range(3):
                    coeff = metric_ref[3 * first + second, row : row + 1, :]
                    result = result + coeff * window[first][second]
            window = [window[1], window[2], None]
            for b in range(PATCH):
                moved = pltpu.roll(result, (span - b * stride) % span, 1) if b else result
                base = (a * PATCH + b) * vpad
                patches[base : base + nvars, :] = moved[:, :lanes].astype(jnp.bfloat16)
        tokens = patches[...].T
        for weight, bias, out in ((weight_b, bias_b, out_b), (weight_a, bias_a, out_a)):
            value = jnp.dot(tokens, weight[...], preferred_element_type=jnp.float32) + bias[...]
            out[q] = value[:cells].astype(jnp.bfloat16)


def encode(chunks, before, after, metric, weights, biases, cells):
    step, nvars, span = chunks[0].shape
    rows_dev = len(chunks) * step // PATCH
    depth, width = weights[0].shape
    out = jax.ShapeDtypeStruct((rows_dev, cells, width), jnp.bfloat16)
    vmem = pl.BlockSpec(memory_space=pltpu.VMEM)
    return pl.pallas_call(
        functools.partial(encode_kernel, len(chunks), cells),
        out_shape=(out, out),
        in_specs=[vmem] * (len(chunks) + 7),
        out_specs=(vmem, vmem),
        scratch_shapes=[pltpu.VMEM((depth, -(-cells // 128) * 128), jnp.bfloat16)],
        compiler_params=pltpu.CompilerParams(vmem_limit_bytes=40 * 1024 * 1024),
        name="encode",
    )(*chunks, before, after, metric, *weights, *biases)


def per_device(cycle_field, cycle_length, metric_weight, patch_weight, patch_bias, owner):
    cycle_rows, nvars, pts_local = cycle_field.shape
    cols_local = metric_weight.shape[2]
    cells = cols_local // PATCH
    stride = -(-(cells + 1) * PATCH // 128) * 128 // PATCH
    nlon = lax.axis_size("lon")
    lon, mp = lax.axis_index("lon"), lax.axis_index("mp")
    bands = lax.axis_size("band")
    kstart = (lon * 2 + mp) * pts_local
    width = patch_weight.shape[1]

    kpad = -nvars % 16
    weight4 = patch_weight.reshape(PATCH, nvars, PATCH, width).transpose(0, 2, 1, 3)
    weight4 = jnp.pad(weight4, ((0, 0), (0, 0), (0, kpad), (0, 0)))
    bias = patch_bias[None, :]
    partner_weight = swap(weight4)
    partner_bias = swap(bias)

    metric = metric_weight.reshape(9, cycle_rows, cells, PATCH).transpose(0, 1, 3, 2)
    metric = jnp.pad(metric, ((0, 0), (0, 0), (0, 0), (0, stride - cells)))
    metric = metric.reshape(9, cycle_rows, PATCH * stride)

    def targets(mp_to):
        return jnp.concatenate(
            [
                column_targets(((lon + d) % nlon * 2 + mp_to) * cols_local, stride)
                for d in range(nlon)
            ]
        )

    own_cols, other_cols = targets(mp), targets(1 - mp)
    step = cycle_rows // CHUNKS
    span = PATCH * stride
    gridded = [None] * CHUNKS
    order = [0, CHUNKS - 1] + list(range(1, CHUNKS - 1))
    messages = {}
    for index, chunk in enumerate(order):
        field = cycle_field[chunk * step : (chunk + 1) * step]
        length = cycle_length[chunk * step : (chunk + 1) * step]
        if index >= 2:
            earlier_chunk = order[index - 2]
            length, messages[earlier_chunk] = lax.optimization_barrier(
                (length, messages[earlier_chunk])
            )
        sent = swap(interpolate(field, length, kstart, other_cols))
        both = interpolate(field, length, kstart, own_cols) + sent
        messages[chunk] = [both[:, :, d * span : (d + 1) * span] for d in range(nlon)]
    for chunk in order:
        total = messages[chunk][0]
        for d in range(1, nlon):
            total = total + lax.ppermute(
                messages[chunk][d], "lon", [(i, (i + d) % nlon) for i in range(nlon)]
            )
        gridded[chunk] = total
    up = [(i, i + 1) for i in range(bands - 1)]
    before = lax.ppermute(gridded[-1][-1:], "band", up)
    after = lax.ppermute(gridded[0][:1], "band", [(b, a) for a, b in up])
    rows_dev = cycle_rows // PATCH
    mine, others = encode(
        gridded,
        before,
        after,
        metric,
        (weight4.reshape(-1, width), partner_weight.reshape(-1, width)),
        (bias, partner_bias),
        cells,
    )
    partner = swap(others)

    dest = owner.reshape(-1)
    count_tok = dest.shape[0]
    capacity = max(2, 2 * count_tok // bands)
    onehot = (dest[:, None] == jnp.arange(bands, dtype=jnp.int32)[None, :]).astype(jnp.int32)
    earlier = jnp.cumsum(onehot, axis=0) - onehot
    slot = jnp.sum(earlier * onehot, axis=1)
    where = (dest * capacity + slot).reshape(rows_dev, 2, cells)
    lower = mp == 0
    halves = jnp.stack(
        [
            jnp.where(lower, where[:, 0], where[:, 1]),
            jnp.where(lower, where[:, 1], where[:, 0]),
        ]
    ).reshape(-1)
    select = (
        halves[None, :] == jnp.arange(bands * capacity, dtype=jnp.int32)[:, None]
    ).astype(jnp.bfloat16)
    tokens = jnp.concatenate([mine.reshape(-1, width), partner.reshape(-1, width)], axis=0)
    outbox = (
        jnp.dot(select, tokens, preferred_element_type=jnp.float32)
        .astype(jnp.bfloat16)
        .reshape(bands, capacity, width)
    )
    inbox = lax.all_to_all(outbox, "band", split_axis=0, concat_axis=0, tiled=True)
    return inbox.reshape(1, 1, bands, capacity, width)


def solution(mesh):
    return jax.shard_map(
        per_device,
        mesh=mesh,
        in_specs=(
            P(("groups", "band"), None, ("lon", "mp")),
            P("band"),
            P(None, "band", ("lon", "mp")),
            P(None, "mp"),
            P("mp"),
            P("band", "lon", None, None),
        ),
        out_specs=P(("groups", "band"), "lon", None, None, "mp"),
        check_vma=False,
    )
```
